32 devices in a mesh: seq: 8 (over z, core), head: 4 (over y, x).
Axes of the slice: x: 2, y: 2, z: 4, core: 2. Of those that a mesh axis runs over, the one named last changes fastest.
Arguments:
- queries: bfloat16 [1024, 2048], P('seq', 'head'), may hold values from -6 to 6
- key_value: bfloat16 [1024, 512], P('seq', 'head'), may hold values from -6 to 6
- grad_out: bfloat16 [1024, 2048], P('seq', 'head'), may hold values from -60 to 60
- ssm_grad: bfloat16 [1024, 2048], P('seq', 'head'), may hold values from -60 to 60
- b_proj: bfloat16 [1024, 128], P('seq'), may hold values from -1.5 to 1.5
- c_proj: bfloat16 [1024, 128], P('seq'), may hold values from -1.5 to 1.5
- decay_log: float32 [32, 1024], P('head', 'seq'), may hold values from -1.2 to 0
- skip_gain: float32 [32], P('head'), may hold values from 1 to 16
Outputs:
- grad_queries: bfloat16 [1024, 2048], P('seq', 'head')
- grad_key_value: bfloat16 [1024, 512], P('seq', 'head')
- grad_ssm_in: bfloat16 [1024, 2048], P('seq', 'head')
The draws below stay inside these ranges and needn't reach their ends.
All inputs are finite; a program needn't handle non-finite values. Where the reference program divides by a largest or mean magnitude, that divisor is 1e-20 or more.
Results may differ from the reference program's by a relative error of at most 0.012.
Values may be sent and summed in bfloat16 or wider, within the bound.
A program may use at most 64 MiB of HBM per device.

```python
import math
import jax
import jax.numpy as jnp
from jax import lax

HEAD_DIM = 128
Q_HEADS = 16
KV_HEADS = 2
TOK_DEV = 128
SEQUENCE_LENGTH = 1024
SSM_HEADS = 32
SSM_DIM = 64
STATE = 128


def attention_pair(key):
    query_key = jax.random.fold_in(key, 101)
    pair_key = jax.random.fold_in(key, 102)
    group = Q_HEADS // KV_HEADS
    queries = jnp.clip(jax.random.normal(query_key, (SEQUENCE_LENGTH, Q_HEADS, HEAD_DIM), jnp.float32), -6.0, 6.0)
    pairs = jnp.clip(jax.random.normal(pair_key, (SEQUENCE_LENGTH, KV_HEADS, 2, HEAD_DIM), jnp.float32), -6.0, 6.0)
    half_length = SEQUENCE_LENGTH // 2
    earlier_keys = jnp.concatenate([jnp.zeros((SEQUENCE_LENGTH - half_length, KV_HEADS, HEAD_DIM), jnp.float32), pairs[:half_length, :, 0]], axis=0)
    earlier_heads = jnp.repeat(earlier_keys, group, axis=1)
    head_number = jnp.arange(Q_HEADS) % group
    chosen_heads = (head_number == 1) | (head_number == 2)
    late_rows = jnp.arange(SEQUENCE_LENGTH) >= SEQUENCE_LENGTH - half_length
    aligned_mask = late_rows[:, None] & chosen_heads[None, :]
    aligned = jnp.clip(0.8 * earlier_heads + 0.6 * queries, -6.0, 6.0)
    queries = jnp.where(aligned_mask[:, :, None], aligned, queries)
    return (queries.reshape(SEQUENCE_LENGTH, Q_HEADS * HEAD_DIM), pairs.reshape(SEQUENCE_LENGTH, KV_HEADS * 2 * HEAD_DIM))


def draw_queries(key, part):
    return attention_pair(key)[0].astype(jnp.bfloat16)


def draw_key_value(key, part):
    return attention_pair(key)[1].astype(jnp.bfloat16)


def cotangent(key, salt, width):
    base = jax.random.fold_in(key, salt)
    noise_key = jax.random.fold_in(base, 1)
    column_key = jax.random.fold_in(base, 2)
    rising = 0.5 * 10.0 ** (jnp.arange(SEQUENCE_LENGTH, dtype=jnp.float32) / SEQUENCE_LENGTH)
    column = jnp.exp(jax.random.uniform(column_key, (width,), jnp.float32, math.log(0.3), math.log(3.0)))
    noise = jnp.clip(jax.random.normal(noise_key, (SEQUENCE_LENGTH, width), jnp.float32), -4.0, 4.0)
    return noise * rising[:, None] * column[None, :]


def draw_grad_out(key, part):
    return cotangent(key, 201, Q_HEADS * HEAD_DIM).astype(jnp.bfloat16)


def draw_ssm_grad(key, part):
    return cotangent(key, 202, SSM_HEADS * SSM_DIM).astype(jnp.bfloat16)


def draw_decay_log(key, part):
    divide_prng_seeds = [jax.random.fold_in(key, 300 + number) for number in range(7)]
    slow_share = 0.5
    is_slow = jax.random.uniform(divide_prng_seeds[0], (SSM_HEADS,), jnp.float32) < slow_share
    slow_rate = jnp.exp(jax.random.uniform(divide_prng_seeds[1], (SSM_HEADS,), jnp.float32, math.log(0.05 / SEQUENCE_LENGTH), math.log(0.3 / SEQUENCE_LENGTH)))
    fast_rate = jnp.exp(jax.random.uniform(divide_prng_seeds[2], (SSM_HEADS,), jnp.float32, math.log(1.0 / 50.0), math.log(1.0 / 30.0)))
    rate = jnp.where(is_slow, slow_rate, fast_rate)
    shard_factor = jnp.exp(jax.random.uniform(divide_prng_seeds[3], (SSM_HEADS, SEQUENCE_LENGTH // TOK_DEV), jnp.float32, math.log(0.5), math.log(2.0)))
    shard_factor = jnp.repeat(shard_factor, TOK_DEV, axis=1)
    rough = jax.random.uniform(divide_prng_seeds[4], (SSM_HEADS, SEQUENCE_LENGTH), jnp.float32, 0.6, 1.6)
    spike_offset = jax.random.randint(divide_prng_seeds[5], (2,), 0, SEQUENCE_LENGTH)
    keeping = jax.random.uniform(divide_prng_seeds[6], (SSM_HEADS, 2), jnp.float32, 0.6, 0.8)
    agreeing_total = (jnp.arange(SEQUENCE_LENGTH)[None, :] == spike_offset[:, None]).astype(jnp.float32)
    return -rate[:, None] * shard_factor * rough + jnp.dot(jnp.log(keeping), agreeing_total)


def shard_levels(rng, shape, pieces, smallest, largest):
    def one(axis_at, shards_of):
        draws = jax.random.uniform(jax.random.fold_in(jax.random.fold_in(rng, 6), axis_at), (shards_of,), jnp.float32, smallest / len(pieces), largest / len(pieces))
        return jnp.repeat(jnp.exp(draws), shape[axis_at] // shards_of).reshape((-1,) + (1,) * (len(shape) - axis_at - 1))

    gain = one(*pieces[0])
    for cut in pieces[1:]:
        gain = gain * one(*cut)
    return gain


def bell_draw(own_key, shape, scale, limit, cuts=(), held_as=jnp.bfloat16):
    factor_of = shard_levels(own_key, shape, cuts, -0.22, 0.18) if cuts else 1.0
    drawn = jax.random.normal(own_key, shape, jnp.float32) * scale * factor_of
    return jnp.minimum(jnp.maximum(drawn, -limit), limit).astype(held_as)


def setup_inputs(seed: int = 0) -> dict:
    arg_keys = jax.random.split(jax.random.key(seed), 9)
    return {
        "queries": draw_queries(jax.random.fold_in(arg_keys[8], 71), 0),
        "key_value": draw_key_value(jax.random.fold_in(arg_keys[8], 71), 0),
        "grad_out": draw_grad_out(jax.random.fold_in(arg_keys[8], 71), 0),
        "ssm_grad": draw_ssm_grad(jax.random.fold_in(arg_keys[8], 71), 0),
        "b_proj": bell_draw(arg_keys[4], (SEQUENCE_LENGTH, STATE), 0.25, 1.5, ((0, 8),)),
        "c_proj": bell_draw(arg_keys[5], (SEQUENCE_LENGTH, STATE), 0.25, 1.5, ((0, 8),)),
        "decay_log": draw_decay_log(jax.random.fold_in(arg_keys[8], 71), 0),
        "skip_gain": jnp.clip(jnp.exp(math.log(16.0) - 2.7725887 * jax.random.uniform(arg_keys[7], (SSM_HEADS,), jnp.float32) ** shard_levels(arg_keys[7], (SSM_HEADS,), ((0, 4),), -0.2, 0.2)), 1.0, 16.0),
    }


epsilon = 1e-06

def head_backward(items):
    query, grad_head, keys, values = items
    score_scale = 1.0 / math.sqrt(HEAD_DIM)
    positions = jnp.arange(SEQUENCE_LENGTH)
    causal = positions[:, None] >= positions[None, :]
    scores = jnp.dot(query, keys.T, preferred_element_type=jnp.float32) * score_scale
    scores = jnp.where(causal, scores, -jnp.inf)
    peak = lax.optimization_barrier(jnp.max(scores, axis=1, keepdims=True))
    log_total = peak + jnp.log(lax.optimization_barrier(jnp.sum(jnp.exp(scores - peak), axis=1, keepdims=True)))
    probs = jnp.exp(scores - log_total)
    probs_b = probs.astype(jnp.bfloat16)
    out_b = jnp.dot(probs_b, values, preferred_element_type=jnp.float32).astype(jnp.bfloat16)
    out_b = lax.optimization_barrier(out_b)
    delta = lax.optimization_barrier(jnp.sum(grad_head.astype(jnp.float32) * out_b.astype(jnp.float32), axis=1, keepdims=True))
    dprob = jnp.dot(grad_head, values.T, preferred_element_type=jnp.float32)
    dscore_b = (probs * (dprob - delta)).astype(jnp.bfloat16)
    grad_q = jnp.dot(dscore_b, keys, preferred_element_type=jnp.float32) * score_scale
    grad_k = jnp.dot(dscore_b.T, query, preferred_element_type=jnp.float32) * score_scale
    grad_v = jnp.dot(probs_b.T, grad_head, preferred_element_type=jnp.float32)
    return (grad_q, grad_k, grad_v)

def reference(queries, key_value, grad_out, ssm_grad, b_proj, c_proj, decay_log, skip_gain):
    group = Q_HEADS // KV_HEADS
    query_heads = queries.reshape(SEQUENCE_LENGTH, Q_HEADS, HEAD_DIM).transpose(1, 0, 2)
    grad_heads = grad_out.reshape(SEQUENCE_LENGTH, Q_HEADS, HEAD_DIM).transpose(1, 0, 2)
    pairs = key_value.reshape(SEQUENCE_LENGTH, KV_HEADS, 2, HEAD_DIM).transpose(1, 2, 0, 3)
    key_heads = jnp.repeat(pairs[:, 0], group, axis=0)
    value_heads = jnp.repeat(pairs[:, 1], group, axis=0)
    grad_q, grad_k, grad_v = lax.map(head_backward, (query_heads, grad_heads, key_heads, value_heads))
    grad_k = grad_k.reshape(KV_HEADS, group, SEQUENCE_LENGTH, HEAD_DIM).sum(axis=1)
    grad_v = grad_v.reshape(KV_HEADS, group, SEQUENCE_LENGTH, HEAD_DIM).sum(axis=1)
    grad_q = grad_q.transpose(1, 0, 2).reshape(SEQUENCE_LENGTH, Q_HEADS * HEAD_DIM)
    grad_kv = jnp.stack([grad_k, grad_v], axis=1).transpose(2, 0, 1, 3).reshape(SEQUENCE_LENGTH, KV_HEADS * 2 * HEAD_DIM)
    grad_in = ssm_grad.reshape(SEQUENCE_LENGTH, SSM_HEADS, SSM_DIM).astype(jnp.float32)
    decay_next = jnp.concatenate([jnp.exp(decay_log[:, 1:]), jnp.zeros((SSM_HEADS, 1), jnp.float32)], axis=1).T

    def backward_step(state, items):
        grad_row, c_row, b_row, next_decay = items
        state = next_decay[:, None, None] * state + grad_row[:, :, None] * c_row[None, None, :]
        result = jnp.einsum('hpn,n->hp', state, b_row, precision=lax.Precision.HIGHEST)
        return (state, result)
    initial = jnp.zeros((SSM_HEADS, SSM_DIM, STATE), jnp.float32)
    _, grad_x = lax.scan(backward_step, initial, (grad_in, c_proj.astype(jnp.float32), b_proj.astype(jnp.float32), decay_next), reverse=True)
    grad_x = grad_x + skip_gain[None, :, None] * grad_in
    grad_x = grad_x.reshape(SEQUENCE_LENGTH, SSM_HEADS * SSM_DIM)
    scaled_q = (grad_q / (jnp.max(jnp.abs(grad_q)) + epsilon)).astype(jnp.bfloat16)
    scaled_kv = (grad_kv / (jnp.max(jnp.abs(grad_kv)) + epsilon)).astype(jnp.bfloat16)
    scaled_x = (grad_x / (jnp.max(jnp.abs(grad_x)) + epsilon)).astype(jnp.bfloat16)
    return (scaled_q, scaled_kv, scaled_x)
```

```python
import functools
import math

import jax
import jax.numpy as jnp
from jax import lax
from jax.experimental import pallas as pl
from jax.experimental.pallas import tpu as pltpu
from jax.sharding import PartitionSpec as P

epsilon = 1e-06
f32 = jnp.float32
bf16 = jnp.bfloat16
MESH = pl.DeviceIdType.MESH


def nn(a, b):
    return jnp.dot(a, b, preferred_element_type=f32)


def nt(a, b, precision=None):
    return lax.dot_general(
        a, b, (((1,), (1,)), ((), ())), preferred_element_type=f32, precision=precision
    )


def kernel(
    n, hn, q_ref, kv_ref, do_ref, dy_ref, b_ref, c_ref, dl_ref, sg_ref,
    gq_ref, gkv_ref, gx_ref,
    kv_all, q_st, q_t, do_st, do_t, score, dkv_out, dkv_in,
    st_out, st_in, dt_out, dt_in, inc_out, inc_in, dx, am_out, am_in, am2_out, am2_in,
    kvs, kvr, dks, dkr, sts, str_, dts, dtr, ins, inr, ams, amr, am2s, am2r,
):
    s = lax.axis_index("seq")
    h = lax.axis_index("head")
    parity = lax.rem(h, 2)
    base = h - parity
    mate = base + 1 - parity
    rows, hd = kv_ref.shape
    heads = q_ref.shape[1] // hd
    cols = heads * rows
    scale = 1.0 / math.sqrt(hd)
    nh, srows = st_out.shape[:2]
    ssm_heads = dl_ref.shape[0]
    width = dy_ref.shape[1]
    sp = width // ssm_heads
    per = hd // sp
    chunk = 2 * rows

    barrier = pltpu.get_barrier_semaphore()

    @pl.loop(0, n)
    def _(d):
        pl.semaphore_signal(barrier, inc=1, device_id=(d, mate), device_id_type=MESH)

        @pl.when(d != s)
        def _():
            pl.semaphore_signal(barrier, inc=1, device_id=(d, h), device_id_type=MESH)

    @pl.loop(0, hn)
    def _(g):
        @pl.when(jnp.logical_and(g != h, g != mate))
        def _():
            pl.semaphore_signal(barrier, inc=1, device_id=(s, g), device_id_type=MESH)

    kv_all[parity, s] = kv_ref[...]

    @pl.when(jnp.logical_and(lax.rem(s, 2) == 0, s + 1 < n))
    def _():
        kv_all[0, s + 1] = jnp.zeros((rows, hd), bf16)
        kv_all[1, s + 1] = jnp.zeros((rows, hd), bf16)

    row_i = lax.broadcasted_iota(jnp.int32, (rows, rows), 0)
    col_i = lax.broadcasted_iota(jnp.int32, (rows, rows), 1)
    tril = jnp.where(col_i <= row_i, 1.0, 0.0).astype(f32)
    decay = dl_ref[...]
    cum = nt(decay, tril, lax.Precision.HIGHEST)
    cum_t = nt(tril, decay, lax.Precision.HIGHEST)
    lane = lax.broadcasted_iota(jnp.int32, (1, hd), 1) // sp

    def spread(x):
        parts = []
        for i in range(ssm_heads // per):
            v = x[:, i * per : i * per + 1]
            for k in range(1, per):
                v = jnp.where(lane == k, x[:, i * per + k : i * per + k + 1], v)
            parts.append(jnp.broadcast_to(v, (x.shape[0], hd)))
        return jnp.concatenate(parts, axis=1)

    dy = dy_ref[...]
    entry = spread(jnp.exp(cum_t))
    scaled = (dy.astype(f32) * entry).astype(bf16)
    c_val = c_ref[...]
    state_t = nn(c_val.T, scaled).astype(bf16)
    for j in range(nh):
        st_out[j] = state_t[j * srows : (j + 1) * srows]
    dt_out[...] = jnp.broadcast_to(jnp.exp(cum[:, rows - 1 : rows]), dt_out.shape)

    pl.semaphore_wait(barrier, 2 * n - 1 + hn - 2)

    def kv_copy(d, g, source, kind):
        return pltpu.make_async_remote_copy(
            src_ref=kv_ref, dst_ref=kv_all.at[kind, source],
            send_sem=kvs.at[g - base, d], recv_sem=kvr.at[kind, source],
            device_id=(d, g), device_id_type=MESH,
        )

    def st_copy(j, source):
        return pltpu.make_async_remote_copy(
            src_ref=st_out.at[j], dst_ref=st_in.at[source],
            send_sem=sts.at[j], recv_sem=str_.at[source],
            device_id=(j, h), device_id_type=MESH,
        )

    def dt_copy(j, source):
        return pltpu.make_async_remote_copy(
            src_ref=dt_out, dst_ref=dt_in.at[source],
            send_sem=dts.at[j], recv_sem=dtr.at[source],
            device_id=(j, h), device_id_type=MESH,
        )

    def inc_copy(d, source):
        return pltpu.make_async_remote_copy(
            src_ref=inc_out.at[d], dst_ref=inc_in.at[source],
            send_sem=ins.at[d], recv_sem=inr.at[source],
            device_id=(d, h), device_id_type=MESH,
        )

    kv_copy(s, mate, s, parity).start()

    @pl.loop(0, nh)
    def _(j):
        @pl.when(j != s)
        def _():
            dt_copy(j, s).start()
            st_copy(j, s).start()

    @pl.loop(s + 1, n)
    def _(d):
        kv_copy(d, h, s, parity).start()
        kv_copy(d, mate, s, parity).start()

    for i in range(heads):
        q_i = q_ref[:, i * hd : (i + 1) * hd]
        d_i = do_ref[:, i * hd : (i + 1) * hd]
        q_st[i * rows : (i + 1) * rows] = q_i
        do_st[i * rows : (i + 1) * rows] = d_i
        q_t[:, i * rows : (i + 1) * rows] = q_i.T
        do_t[:, i * rows : (i + 1) * rows] = d_i.T

    pair = nt(b_ref[...], c_val)
    upper = col_i >= row_i
    for i in range(ssm_heads // per):
        dy_i = dy[:, i * hd : (i + 1) * hd]
        total = None
        gain = None
        for k in range(per):
            a = i * per + k
            span = jnp.where(upper, cum[a : a + 1, :] - cum_t[:, a : a + 1], -1e30)
            w = (jnp.exp(span) * pair).astype(bf16)
            r = nn(w, dy_i)
            total = r if k == 0 else jnp.where(lane == k, r, total)
            gain = (
                jnp.full((1, hd), sg_ref[a], f32) if k == 0 else jnp.where(lane == k, sg_ref[a], gain)
            )
        dx[:, i * hd : (i + 1) * hd] = total + gain * dy_i.astype(f32)

    @pl.when(s < nh)
    def _():
        st_in[s] = st_out[jnp.minimum(s, nh - 1)]
        dt_in[s] = dt_out[...]

        def one(step, inc):
            i = n - 1 - step
            inc_out[i] = inc.astype(bf16)

            @pl.when(i != s)
            def _():
                inc_copy(i, s).start()
                st_copy(jnp.minimum(s, nh - 1), i).wait_recv()
                dt_copy(jnp.minimum(s, nh - 1), i).wait_recv()

            d = dt_in[i]
            parts = []
            for a in range(ssm_heads // per):
                v = d[a * per : a * per + 1]
                for k in range(1, per):
                    v = jnp.where(lane == k, d[a * per + k : a * per + k + 1], v)
                parts.append(v)
            return st_in[i].astype(f32) + jnp.concatenate(parts, axis=1) * inc

        lax.fori_loop(0, n, one, jnp.zeros((srows, width), f32))
        inc_in[jnp.minimum(s, nh - 1)] = inc_out[s]

    chunks = s // 2 + 1
    key_i = lax.broadcasted_iota(jnp.int32, (chunk, cols), 0)
    query_i = s * rows + lax.rem(lax.broadcasted_iota(jnp.int32, (1, cols), 1), rows)

    def await_kind(kind, j):
        for k in range(2):
            blk = 2 * j + k

            @pl.when(jnp.logical_and(blk <= s, jnp.logical_or(blk != s, parity != kind)))
            def _():
                kv_copy(s, h, blk, kind).wait_recv()

    def load(kind, j):
        return kv_all[kind, pl.ds(2 * j, 2)].reshape(chunk, hd)

    def first(j, top):
        await_kind(0, j)
        sc = nn(load(0, j), q_t[...]) * scale
        sc = jnp.where(key_i + j * chunk <= query_i, sc, -1e30)
        score[j] = sc
        return jnp.maximum(top, jnp.max(sc, axis=0, keepdims=True))

    top = lax.fori_loop(0, chunks, first, jnp.full((1, cols), -1e30, f32))

    def second(j, total):
        e = jnp.exp(score[j] - top)
        score[j] = e
        return total + jnp.sum(e, axis=0, keepdims=True)

    total = lax.fori_loop(0, chunks, second, jnp.zeros((1, cols), f32))
    inv = 1.0 / total

    def dkv_copy(kind, blk, source, member):
        return pltpu.make_async_remote_copy(
            src_ref=dkv_out.at[kind, blk], dst_ref=dkv_in.at[source, member],
            send_sem=dks.at[kind, blk], recv_sem=dkr.at[source, member],
            device_id=(blk, base + kind), device_id_type=MESH,
        )

    def other(kind, blk):
        return jnp.logical_and(blk <= s, jnp.logical_or(blk != s, parity != kind))

    def send_grads(kind, j, val):
        for k in range(2):
            blk = 2 * j + k
            dkv_out[kind, blk] = val[k * rows : (k + 1) * rows].astype(bf16)

            @pl.when(other(kind, blk))
            def _():
                dkv_copy(kind, blk, s, parity).start()

    def third(j, out):
        await_kind(1, j)
        p = score[j] * inv
        score[j] = p
        pb = p.astype(bf16)
        send_grads(1, j, nn(pb, do_st[...]))
        return out + nn(load(1, j).T, pb)

    out_t = lax.fori_loop(0, chunks, third, jnp.zeros((hd, cols), f32))
    delta = jnp.sum(do_t[...].astype(f32) * out_t.astype(bf16).astype(f32), axis=0, keepdims=True)

    def fourth(j, dq):
        dp = nn(load(1, j), do_t[...])
        ds = (score[j] * (dp - delta)).astype(bf16)
        send_grads(0, j, nn(ds, q_st[...]) * scale)
        return dq + nn(load(0, j).T, ds)

    dq_t = lax.fori_loop(0, chunks, fourth, jnp.zeros((hd, cols), f32)) * scale

    @pl.loop(0, nh)
    def _(j):
        @pl.when(j != s)
        def _():
            inc_copy(s, j).wait_recv()

    carried = nn(b_ref[...], inc_in[...].reshape(nh * srows, width))
    tail = spread(jnp.exp(cum_t[rows - 1 : rows, :] - cum_t))
    dx_full = dx[...] + carried * tail
    dx[...] = dx_full

    def peak(x):
        return jnp.max(jnp.max(jnp.abs(x), axis=0, keepdims=True), axis=1, keepdims=True)

    peak_q = peak(dq_t)
    peak_x = peak(dx_full)

    def add_source(i, acc):
        for m in range(2):
            @pl.when(jnp.logical_or(i != s, parity != m))
            def _():
                dkv_copy(parity, s, i, m).wait_recv()

            acc = acc + dkv_in[i, m].astype(f32)
        return acc

    dkv_in[s, parity] = dkv_out[parity, s]
    kv_grad = lax.fori_loop(s, n, add_source, jnp.zeros((rows, hd), f32))
    peak_kv = peak(kv_grad)

    sub = lax.broadcasted_iota(jnp.int32, am_out.shape, 0)
    mine = jnp.where(sub == 0, peak_q, jnp.where(sub == 1, peak_kv, peak_x))
    am_out[...] = mine
    am_in[s] = mine

    def am_copy(d, source):
        return pltpu.make_async_remote_copy(
            src_ref=am_out, dst_ref=am_in.at[source],
            send_sem=ams.at[d], recv_sem=amr.at[source],
            device_id=(d, h), device_id_type=MESH,
        )

    def am2_copy(g, source):
        return pltpu.make_async_remote_copy(
            src_ref=am2_out, dst_ref=am2_in.at[source],
            send_sem=am2s.at[g], recv_sem=am2r.at[source],
            device_id=(s, g), device_id_type=MESH,
        )

    def each_other(count, me, act):
        @pl.loop(0, count)
        def _(d):
            @pl.when(d != me)
            def _():
                act(d)

    each_other(n, s, lambda d: am_copy(d, s).start())
    each_other(n, s, lambda d: am_copy(s, d).wait_recv())
    column = jnp.max(am_in[...], axis=0)
    am2_out[...] = column
    am2_in[h] = column
    each_other(hn, h, lambda g: am2_copy(g, h).start())
    each_other(hn, h, lambda g: am2_copy(h, g).wait_recv())
    inverse = 1.0 / (jnp.max(am2_in[...], axis=0) + epsilon)

    scaled_q = dq_t * inverse[0:1, 0:1]
    for i in range(heads):
        gq_ref[:, i * hd : (i + 1) * hd] = scaled_q[:, i * rows : (i + 1) * rows].T.astype(bf16)
    gkv_ref[...] = (kv_grad * inverse[1:2, 0:1]).astype(bf16)
    gx_ref[...] = (dx[...] * inverse[2:3, 0:1]).astype(bf16)

    kv_copy(s, mate, s, parity).wait_send()

    @pl.loop(s + 1, n)
    def _(d):
        kv_copy(d, h, s, parity).wait_send()
        kv_copy(d, mate, s, parity).wait_send()

    @pl.loop(0, nh)
    def _(j):
        @pl.when(j != s)
        def _():
            st_copy(j, s).wait_send()
            dt_copy(j, s).wait_send()

    @pl.when(s < nh)
    def _():
        each_other(n, s, lambda d: inc_copy(d, s).wait_send())

    @pl.loop(0, s + 1)
    def _(blk):
        for kind in range(2):
            @pl.when(other(kind, blk))
            def _():
                dkv_copy(kind, blk, s, parity).wait_send()

    each_other(n, s, lambda d: am_copy(d, s).wait_send())
    each_other(hn, h, lambda g: am2_copy(g, h).wait_send())


def on_device(queries, key_value, grad_out, ssm_grad, b_proj, c_proj, decay_log, skip_gain):
    n = lax.axis_size("seq")
    hn = lax.axis_size("head")
    rows, hd = key_value.shape
    heads = queries.shape[1] // hd
    cols = heads * rows
    width = ssm_grad.shape[1]
    state = b_proj.shape[1]
    ssm_heads = decay_log.shape[0]
    nh = min(n, state // 16)
    srows = state // nh
    vmem = pltpu.VMEM
    dma = pltpu.SemaphoreType.DMA
    full = pl.BlockSpec(memory_space=pltpu.VMEM)
    return pl.pallas_call(
        functools.partial(kernel, n, hn),
        out_shape=(
            jax.ShapeDtypeStruct(queries.shape, bf16),
            jax.ShapeDtypeStruct(key_value.shape, bf16),
            jax.ShapeDtypeStruct(ssm_grad.shape, bf16),
        ),
        in_specs=[full] * 7 + [pl.BlockSpec(memory_space=pltpu.SMEM)],
        out_specs=(full, full, full),
        scratch_shapes=[
            vmem((2, n, rows, hd), bf16),
            vmem((cols, hd), bf16),
            vmem((hd, cols), bf16),
            vmem((cols, hd), bf16),
            vmem((hd, cols), bf16),
            vmem((n // 2, 2 * rows, cols), f32),
            vmem((2, n, rows, hd), bf16),
            vmem((n, 2, rows, hd), bf16),
            vmem((nh, srows, width), bf16),
            vmem((n, srows, width), bf16),
            vmem((ssm_heads, hd), f32),
            vmem((n, ssm_heads, hd), f32),
            vmem((n, srows, width), bf16),
            vmem((nh, srows, width), bf16),
            vmem((rows, width), f32),
            vmem((8, hd), f32),
            vmem((n, 8, hd), f32),
            vmem((8, hd), f32),
            vmem((hn, 8, hd), f32),
            dma((2, n)), dma((2, n)),
            dma((2, n)), dma((n, 2)),
            dma((nh,)), dma((n,)),
            dma((nh,)), dma((n,)),
            dma((n,)), dma((nh,)),
            dma((n,)), dma((n,)),
            dma((hn,)), dma((hn,)),
        ],
        compiler_params=pltpu.CompilerParams(
            collective_id=0, has_side_effects=True, vmem_limit_bytes=48 * 1024 * 1024
        ),
    )(queries, key_value, grad_out, ssm_grad, b_proj, c_proj, decay_log, skip_gain)


def solution(mesh):
    return jax.shard_map(
        on_device,
        mesh=mesh,
        in_specs=(
            P("seq", "head"),
            P("seq", "head"),
            P("seq", "head"),
            P("seq", "head"),
            P("seq", None),
            P("seq", None),
            P("head", "seq"),
            P("head"),
        ),
        out_specs=(P("seq", "head"), P("seq", "head"), P("seq", "head")),
        check_vma=False,
    )
```

```python
import functools
import math

import jax
import jax.numpy as jnp
from jax import lax
from jax.experimental import pallas as pl
from jax.experimental.pallas import tpu as pltpu
from jax.sharding import PartitionSpec as P

epsilon = 1e-06
f32 = jnp.float32
bf16 = jnp.bfloat16
MESH = pl.DeviceIdType.MESH


def nn(a, b):
    return jnp.dot(a, b, preferred_element_type=f32)


def nt(a, b, precision=None):
    return lax.dot_general(
        a, b, (((1,), (1,)), ((), ())), preferred_element_type=f32, precision=precision
    )


def kernel(
    n, hn, flat, q_hbm, kv_hbm, do_hbm, dy_hbm, b_hbm, c_hbm, dl_hbm, sg_ref,
    gq_ref, gkv_ref, gx_ref,
    q_ref, kv_ref, do_ref, dy_ref, b_ref, c_ref, dl_ref,
    kv_all, q_st, q_t, do_st, do_t, score, dkv_out, dkv_in,
    st_out, st_in, dt_out, dt_in, inc_out, inc_in, dx, am_out, am_in, am2_out, am2_in,
    loads, fws, kvs, kvr, dks, dkr, sts, str_, dts, dtr, ins, inr, ams, amr, am2s, am2r,
):
    s = lax.axis_index("seq")
    h = lax.axis_index("head")
    parity = lax.rem(h, 2)
    base = h - parity
    mate = base + 1 - parity
    rows, hd = kv_ref.shape
    heads = q_ref.shape[1] // hd
    cols = heads * rows
    scale = 1.0 / math.sqrt(hd)
    nh, srows = st_out.shape[:2]
    ssm_heads = dl_ref.shape[0]
    width = dy_ref.shape[1]
    sp = width // ssm_heads
    per = hd // sp
    chunk = 2 * rows
    core = lax.rem(s, 2)
    chip = s // 2
    sibling = s + 1 - 2 * core

    fetch = [
        pltpu.make_async_copy(a, b, loads.at[i])
        for i, (a, b) in enumerate((
            (dl_hbm, dl_ref), (dy_hbm, dy_ref), (c_hbm, c_ref), (kv_hbm, kv_ref),
            (b_hbm, b_ref), (q_hbm, q_ref), (do_hbm, do_ref),
        ))
    ]
    for copy in fetch:
        copy.start()
    barrier = pltpu.get_barrier_semaphore()

    if flat:

        @pl.loop(0, n)
        def _(d):
            @pl.loop(0, hn)
            def _(g):
                @pl.when(jnp.logical_or(d != s, g != h))
                def _():
                    pl.semaphore_signal(barrier, inc=1, device_id=(d, g), device_id_type=MESH)

        greeted = n * hn - 1
    else:

        @pl.loop(0, n)
        def _(d):
            pl.semaphore_signal(barrier, inc=1, device_id=(d, mate), device_id_type=MESH)

            @pl.when(d != s)
            def _():
                pl.semaphore_signal(barrier, inc=1, device_id=(d, h), device_id_type=MESH)

        @pl.loop(0, hn)
        def _(g):
            @pl.when(jnp.logical_and(g != h, g != mate))
            def _():
                pl.semaphore_signal(barrier, inc=1, device_id=(s, g), device_id_type=MESH)

        greeted = 2 * n - 1 + hn - 2

    for copy in fetch[:4]:
        copy.wait()
    kv_all[parity, s] = kv_ref[...]

    @pl.when(jnp.logical_and(lax.rem(s, 2) == 0, s + 1 < n))
    def _():
        kv_all[0, s + 1] = jnp.zeros((rows, hd), bf16)
        kv_all[1, s + 1] = jnp.zeros((rows, hd), bf16)

    row_i = lax.broadcasted_iota(jnp.int32, (rows, rows), 0)
    col_i = lax.broadcasted_iota(jnp.int32, (rows, rows), 1)
    tril = jnp.where(col_i <= row_i, 1.0, 0.0).astype(f32)
    decay = dl_ref[...]
    cum = nt(decay, tril, lax.Precision.HIGHEST)
    cum_t = nt(tril, decay, lax.Precision.HIGHEST)
    lane = lax.broadcasted_iota(jnp.int32, (1, hd), 1) // sp

    def spread(x):
        parts = []
        for i in range(ssm_heads // per):
            v = x[:, i * per : i * per + 1]
            for k in range(1, per):
                v = jnp.where(lane == k, x[:, i * per + k : i * per + k + 1], v)
            parts.append(jnp.broadcast_to(v, (x.shape[0], hd)))
        return jnp.concatenate(parts, axis=1)

    dy = dy_ref[...]
    entry = spread(jnp.exp(cum_t))
    scaled = (dy.astype(f32) * entry).astype(bf16)
    c_val = c_ref[...]
    state_t = nn(c_val.T, scaled).astype(bf16)
    for j in range(nh):
        st_out[j] = state_t[j * srows : (j + 1) * srows]
    dt_out[...] = jnp.broadcast_to(jnp.exp(cum[:, rows - 1 : rows]), dt_out.shape)

    pl.semaphore_wait(barrier, greeted)

    def kv_copy(d, g, source, kind):
        return pltpu.make_async_remote_copy(
            src_ref=kv_ref, dst_ref=kv_all.at[kind, source],
            send_sem=kvs.at[g - base, d], recv_sem=kvr.at[kind, source],
            device_id=(d, g), device_id_type=MESH,
        )

    def forward(source, kind):
        return pltpu.make_async_remote_copy(
            src_ref=kv_all.at[kind, source], dst_ref=kv_all.at[kind, source],
            send_sem=fws.at[kind, source], recv_sem=kvr.at[kind, source],
            device_id=(sibling, h), device_id_type=MESH,
        )

    def st_copy(j, source):
        return pltpu.make_async_remote_copy(
            src_ref=st_out.at[j], dst_ref=st_in.at[source],
            send_sem=sts.at[j], recv_sem=str_.at[source],
            device_id=(j, h), device_id_type=MESH,
        )

    def dt_copy(j, source):
        return pltpu.make_async_remote_copy(
            src_ref=dt_out, dst_ref=dt_in.at[source],
            send_sem=dts.at[j], recv_sem=dtr.at[source],
            device_id=(j, h), device_id_type=MESH,
        )

    def inc_copy(d, source):
        return pltpu.make_async_remote_copy(
            src_ref=inc_out.at[d], dst_ref=inc_in.at[source],
            send_sem=ins.at[d], recv_sem=inr.at[source],
            device_id=(d, h), device_id_type=MESH,
        )

    @pl.loop(chip + 1, n // 2)
    def _(z):
        kv_copy(2 * z + core, h, s, parity).start()
        kv_copy(2 * z + core, mate, s, parity).start()

    kv_copy(s, mate, s, parity).start()

    @pl.when(core == 0)
    def _():
        kv_copy(sibling, h, s, parity).start()

    @pl.loop(0, nh)
    def _(j):
        @pl.when(j != s)
        def _():
            dt_copy(j, s).start()
            st_copy(j, s).start()

    for copy in fetch[4:]:
        copy.wait()
    for i in range(heads):
        q_i = q_ref[:, i * hd : (i + 1) * hd]
        d_i = do_ref[:, i * hd : (i + 1) * hd]
        q_st[i * rows : (i + 1) * rows] = q_i
        do_st[i * rows : (i + 1) * rows] = d_i
        q_t[:, i * rows : (i + 1) * rows] = q_i.T
        do_t[:, i * rows : (i + 1) * rows] = d_i.T

    pair = nt(b_ref[...], c_val)
    upper = col_i >= row_i
    for i in range(ssm_heads // per):
        dy_i = dy[:, i * hd : (i + 1) * hd]
        total = None
        gain = None
        for k in range(per):
            a = i * per + k
            span = jnp.where(upper, cum[a : a + 1, :] - cum_t[:, a : a + 1], -1e30)
            w = (jnp.exp(span) * pair).astype(bf16)
            r = nn(w, dy_i)
            total = r if k == 0 else jnp.where(lane == k, r, total)
            gain = (
                jnp.full((1, hd), sg_ref[a], f32) if k == 0 else jnp.where(lane == k, sg_ref[a], gain)
            )
        dx[:, i * hd : (i + 1) * hd] = total + gain * dy_i.astype(f32)

    chunks = s // 2 + 1
    key_i = lax.broadcasted_iota(jnp.int32, (chunk, cols), 0)
    query_i = s * rows + lax.rem(lax.broadcasted_iota(jnp.int32, (1, cols), 1), rows)

    def pass_on(kind):
        @pl.loop(0, chip)
        def _(z):
            kv_copy(s, h, 2 * z + core, kind).wait_recv()
            forward(2 * z + core, kind).start()

        @pl.when(parity != kind)
        def _():
            kv_copy(s, h, s, kind).wait_recv()

            @pl.when(core == 0)
            def _():
                forward(s, kind).start()

    def await_kind(kind, j):
        blk = 2 * j + 1 - core

        @pl.when(blk < s)
        def _():
            kv_copy(s, h, blk, kind).wait_recv()

    def load(kind, j):
        return kv_all[kind, pl.ds(2 * j, 2)].reshape(chunk, hd)

    def first(j, top):
        await_kind(0, j)
        sc = nn(load(0, j), q_t[...]) * scale
        sc = jnp.where(key_i + j * chunk <= query_i, sc, -1e30)
        score[j] = sc
        return jnp.maximum(top, jnp.max(sc, axis=0, keepdims=True))

    pass_on(0)
    top = lax.fori_loop(0, chunks, first, jnp.full((1, cols), -1e30, f32))
    pass_on(1)

    @pl.when(s < nh)
    def _():
        st_in[s] = st_out[jnp.minimum(s, nh - 1)]
        dt_in[s] = dt_out[...]

        def one(step, inc):
            i = n - 1 - step
            inc_out[i] = inc.astype(bf16)

            @pl.when(i != s)
            def _():
                inc_copy(i, s).start()
                st_copy(jnp.minimum(s, nh - 1), i).wait_recv()
                dt_copy(jnp.minimum(s, nh - 1), i).wait_recv()

            d = dt_in[i]
            parts = []
            for a in range(ssm_heads // per):
                v = d[a * per : a * per + 1]
                for k in range(1, per):
                    v = jnp.where(lane == k, d[a * per + k : a * per + k + 1], v)
                parts.append(v)
            return st_in[i].astype(f32) + jnp.concatenate(parts, axis=1) * inc

        lax.fori_loop(0, n, one, jnp.zeros((srows, width), f32))
        inc_in[jnp.minimum(s, nh - 1)] = inc_out[s]

    def second(j, total):
        e = jnp.exp(score[j] - top)
        score[j] = e
        return total + jnp.sum(e, axis=0, keepdims=True)

    total = lax.fori_loop(0, chunks, second, jnp.zeros((1, cols), f32))
    inv = 1.0 / total

    def dkv_copy(kind, blk, source, member):
        return pltpu.make_async_remote_copy(
            src_ref=dkv_out.at[kind, blk], dst_ref=dkv_in.at[source, member],
            send_sem=dks.at[kind, blk], recv_sem=dkr.at[source, member],
            device_id=(blk, base + kind), device_id_type=MESH,
        )

    def other(kind, blk):
        return jnp.logical_and(blk <= s, jnp.logical_or(blk != s, parity != kind))

    def send_grads(kind, j, val):
        for k in range(2):
            blk = 2 * j + k
            dkv_out[kind, blk] = val[k * rows : (k + 1) * rows].astype(bf16)

            @pl.when(other(kind, blk))
            def _():
                dkv_copy(kind, blk, s, parity).start()

    def third(j, out):
        await_kind(1, j)
        p = score[j] * inv
        score[j] = p
        pb = p.astype(bf16)
        send_grads(1, j, nn(pb, do_st[...]))
        return out + nn(load(1, j).T, pb)

    out_t = lax.fori_loop(0, chunks, third, jnp.zeros((hd, cols), f32))
    delta = jnp.sum(do_t[...].astype(f32) * out_t.astype(bf16).astype(f32), axis=0, keepdims=True)

    def fourth(j, dq):
        dp = nn(load(1, j), do_t[...])
        ds = (score[j] * (dp - delta)).astype(bf16)
        send_grads(0, j, nn(ds, q_st[...]) * scale)
        return dq + nn(load(0, j).T, ds)

    dq_t = lax.fori_loop(0, chunks, fourth, jnp.zeros((hd, cols), f32)) * scale

    @pl.loop(0, nh)
    def _(j):
        @pl.when(j != s)
        def _():
            inc_copy(s, j).wait_recv()

    carried = nn(b_ref[...], inc_in[...].reshape(nh * srows, width))
    tail = spread(jnp.exp(cum_t[rows - 1 : rows, :] - cum_t))
    dx_full = dx[...] + carried * tail
    dx[...] = dx_full

    def peak(x):
        return jnp.max(jnp.max(jnp.abs(x), axis=0, keepdims=True), axis=1, keepdims=True)

    peak_q = peak(dq_t)
    peak_x = peak(dx_full)

    def add_source(i, acc):
        for m in range(2):
            @pl.when(jnp.logical_or(i != s, parity != m))
            def _():
                dkv_copy(parity, s, i, m).wait_recv()

            acc = acc + dkv_in[i, m].astype(f32)
        return acc

    dkv_in[s, parity] = dkv_out[parity, s]
    kv_grad = lax.fori_loop(s, n, add_source, jnp.zeros((rows, hd), f32))
    peak_kv = peak(kv_grad)

    sub = lax.broadcasted_iota(jnp.int32, am_out.shape, 0)
    mine = jnp.where(sub == 0, peak_q, jnp.where(sub == 1, peak_kv, peak_x))
    am_out[...] = mine
    am_in[s * hn + h if flat else s] = mine

    def am_all(d, g, e, f):
        return pltpu.make_async_remote_copy(
            src_ref=am_out, dst_ref=am_in.at[e * hn + f],
            send_sem=ams.at[d * hn + g], recv_sem=amr.at[e * hn + f],
            device_id=(d, g), device_id_type=MESH,
        )

    def all_others(act):
        @pl.loop(0, n)
        def _(d):
            @pl.loop(0, hn)
            def _(g):
                @pl.when(jnp.logical_or(d != s, g != h))
                def _():
                    act(d, g)

    def am_copy(d, source):
        return pltpu.make_async_remote_copy(
            src_ref=am_out, dst_ref=am_in.at[source],
            send_sem=ams.at[d], recv_sem=amr.at[source],
            device_id=(d, h), device_id_type=MESH,
        )

    def am2_copy(g, source):
        return pltpu.make_async_remote_copy(
            src_ref=am2_out, dst_ref=am2_in.at[source],
            send_sem=am2s.at[g], recv_sem=am2r.at[source],
            device_id=(s, g), device_id_type=MESH,
        )

    def each_other(count, me, act):
        @pl.loop(0, count)
        def _(d):
            @pl.when(d != me)
            def _():
                act(d)

    if flat:
        all_others(lambda d, g: am_all(d, g, s, h).start())
        all_others(lambda d, g: am_all(s, h, d, g).wait_recv())
        inverse = 1.0 / (jnp.max(am_in[...], axis=0) + epsilon)
    else:
        each_other(n, s, lambda d: am_copy(d, s).start())
        each_other(n, s, lambda d: am_copy(s, d).wait_recv())
        column = jnp.max(am_in[...], axis=0)
        am2_out[...] = column
        am2_in[h] = column
        each_other(hn, h, lambda g: am2_copy(g, h).start())
        each_other(hn, h, lambda g: am2_copy(h, g).wait_recv())
        inverse = 1.0 / (jnp.max(am2_in[...], axis=0) + epsilon)

    scaled_q = dq_t * inverse[0:1, 0:1]
    for i in range(heads):
        gq_ref[:, i * hd : (i + 1) * hd] = scaled_q[:, i * rows : (i + 1) * rows].T.astype(bf16)
    gkv_ref[...] = (kv_grad * inverse[1:2, 0:1]).astype(bf16)
    gx_ref[...] = (dx[...] * inverse[2:3, 0:1]).astype(bf16)

    kv_copy(s, mate, s, parity).wait_send()

    @pl.when(core == 0)
    def _():
        kv_copy(sibling, h, s, parity).wait_send()
        forward(s, 1 - parity).wait_send()

    @pl.loop(chip + 1, n // 2)
    def _(z):
        kv_copy(2 * z + core, h, s, parity).wait_send()
        kv_copy(2 * z + core, mate, s, parity).wait_send()

    @pl.loop(0, chip)
    def _(z):
        forward(2 * z + core, 0).wait_send()
        forward(2 * z + core, 1).wait_send()

    @pl.loop(0, nh)
    def _(j):
        @pl.when(j != s)
        def _():
            st_copy(j, s).wait_send()
            dt_copy(j, s).wait_send()

    @pl.when(s < nh)
    def _():
        each_other(n, s, lambda d: inc_copy(d, s).wait_send())

    @pl.loop(0, s + 1)
    def _(blk):
        for kind in range(2):
            @pl.when(other(kind, blk))
            def _():
                dkv_copy(kind, blk, s, parity).wait_send()

    if flat:
        all_others(lambda d, g: am_all(d, g, s, h).wait_send())
    else:
        each_other(n, s, lambda d: am_copy(d, s).wait_send())
        each_other(hn, h, lambda g: am2_copy(g, h).wait_send())


def hand_over(a, b, c, x, y, z, sems):
    copies = [
        pltpu.make_async_copy(i, o, sems.at[k]) for k, (i, o) in enumerate(((a, x), (b, y), (c, z)))
    ]
    for copy in copies:
        copy.start()
    for copy in copies:
        copy.wait()


def on_device(queries, key_value, grad_out, ssm_grad, b_proj, c_proj, decay_log, skip_gain):
    n = lax.axis_size("seq")
    hn = lax.axis_size("head")
    rows, hd = key_value.shape
    heads = queries.shape[1] // hd
    cols = heads * rows
    width = ssm_grad.shape[1]
    state = b_proj.shape[1]
    ssm_heads = decay_log.shape[0]
    nh = min(n, state // 16)
    srows = state // nh
    vmem = pltpu.VMEM
    dma = pltpu.SemaphoreType.DMA
    full = pl.BlockSpec(memory_space=pltpu.VMEM)
    far = pl.BlockSpec(memory_space=pltpu.HBM)
    flat = n * hn <= 64
    groups = n * hn if flat else n
    grads = pl.pallas_call(
        functools.partial(kernel, n, hn, flat),
        out_shape=(
            jax.ShapeDtypeStruct(queries.shape, bf16),
            jax.ShapeDtypeStruct(key_value.shape, bf16),
            jax.ShapeDtypeStruct(ssm_grad.shape, bf16),
        ),
        in_specs=[far] * 7 + [pl.BlockSpec(memory_space=pltpu.SMEM)],
        out_specs=(full, full, full),
        scratch_shapes=[
            *(
                vmem(a.shape, a.dtype)
                for a in (queries, key_value, grad_out, ssm_grad, b_proj, c_proj, decay_log)
            ),
            vmem((2, n, rows, hd), bf16),
            vmem((cols, hd), bf16),
            vmem((hd, cols), bf16),
            vmem((cols, hd), bf16),
            vmem((hd, cols), bf16),
            vmem((n // 2, 2 * rows, cols), f32),
            vmem((2, n, rows, hd), bf16),
            vmem((n, 2, rows, hd), bf16),
            vmem((nh, srows, width), bf16),
            vmem((n, srows, width), bf16),
            vmem((ssm_heads, hd), f32),
            vmem((n, ssm_heads, hd), f32),
            vmem((n, srows, width), bf16),
            vmem((nh, srows, width), bf16),
            vmem((rows, width), f32),
            vmem((8, hd), f32),
            vmem((groups, 8, hd), f32),
            vmem((8, hd), f32),
            vmem((hn, 8, hd), f32),
            dma((7,)), dma((2, n)),
            dma((2, n)), dma((2, n)),
            dma((2, n)), dma((n, 2)),
            dma((nh,)), dma((n,)),
            dma((nh,)), dma((n,)),
            dma((n,)), dma((nh,)),
            dma((groups,)), dma((groups,)),
            dma((hn,)), dma((hn,)),
        ],
        compiler_params=pltpu.CompilerParams(
            collective_id=0, has_side_effects=True, vmem_limit_bytes=56 * 1024 * 1024
        ),
    )(queries, key_value, grad_out, ssm_grad, b_proj, c_proj, decay_log, skip_gain)
    return pl.pallas_call(
        hand_over,
        out_shape=tuple(jax.ShapeDtypeStruct(a.shape, a.dtype) for a in grads),
        in_specs=[far] * 3,
        out_specs=(far,) * 3,
        scratch_shapes=[dma((3,))],
        compiler_params=pltpu.CompilerParams(vmem_limit_bytes=56 * 1024 * 1024),
    )(*grads)


def solution(mesh):
    return jax.shard_map(
        on_device,
        mesh=mesh,
        in_specs=(
            P("seq", "head"),
            P("seq", "head"),
            P("seq", "head"),
            P("seq", "head"),
            P("seq", None),
            P("seq", None),
            P("head", "seq"),
            P("head"),
        ),
        out_specs=(P("seq", "head"), P("seq", "head"), P("seq", "head")),
        check_vma=False,
    )
```

```python
import functools
import math

import jax
import jax.numpy as jnp
from jax import lax
from jax.experimental import pallas as pl
from jax.experimental.pallas import tpu as pltpu
from jax.sharding import PartitionSpec as P

epsilon = 1e-06
f32 = jnp.float32
bf16 = jnp.bfloat16
MESH = pl.DeviceIdType.MESH


def nn(a, b):
    return jnp.dot(a, b, preferred_element_type=f32)


def nt(a, b, precision=None):
    return lax.dot_general(
        a, b, (((1,), (1,)), ((), ())), preferred_element_type=f32, precision=precision
    )


def kernel(
    n, hn, q_hbm, kv_hbm, do_hbm, dy_hbm, b_hbm, c_hbm, dl_hbm, sg_ref,
    gq_ref, gkv_ref, gx_ref,
    q_ref, kv_ref, do_ref, dy_ref, b_ref, c_ref, dl_ref,
    kv_all, q_st, q_t, do_st, do_t, score, dkv_out, dkv_in, dkv_part, pair_in,
    st_out, st_in, inc_out, inc_in, dx, am_out, am_in, am2_out, am2_in,
    loads, fws, kvs, kvr, dks, dkr, prs, prr, sts, str_, ins, inr, ams, amr, am2s, am2r,
):
    s = lax.axis_index("seq")
    h = lax.axis_index("head")
    parity = lax.rem(h, 2)
    base = h - parity
    mate = base + 1 - parity
    rows, hd = kv_ref.shape
    heads = q_ref.shape[1] // hd
    cols = heads * rows
    scale = 1.0 / math.sqrt(hd)
    nh, srows = st_out.shape[:2]
    ssm_heads = dl_ref.shape[0]
    width = dy_ref.shape[1]
    sp = width // ssm_heads
    per = hd // sp
    chunk = 2 * rows
    core = lax.rem(s, 2)
    chip = s // 2
    sibling = s + 1 - 2 * core

    fetch = [
        pltpu.make_async_copy(a, b, loads.at[i])
        for i, (a, b) in enumerate((
            (dl_hbm, dl_ref), (dy_hbm, dy_ref), (c_hbm, c_ref), (kv_hbm, kv_ref),
            (b_hbm, b_ref), (q_hbm, q_ref), (do_hbm, do_ref),
        ))
    ]
    for copy in fetch:
        copy.start()
    barrier = pltpu.get_barrier_semaphore()

    for k in range(1, n):
        pl.semaphore_signal(
            barrier, inc=1, device_id=(lax.rem(s + k, n), h), device_id_type=MESH
        )
    for k in range(0, n, 2):
        pl.semaphore_signal(
            barrier, inc=1, device_id=(lax.rem(s + k, n), mate), device_id_type=MESH
        )
    for k in range(2, hn):
        g = lax.rem(base + k, hn)
        pl.semaphore_signal(barrier, inc=1, device_id=(s, g), device_id_type=MESH)

    def settle(ref, sem):
        pltpu.make_async_copy(ref, ref, sem).wait()

    for copy in fetch[:4]:
        copy.wait()
    kv_all[parity, s] = kv_ref[...]

    @pl.when(jnp.logical_and(lax.rem(s, 2) == 0, s + 1 < n))
    def _():
        kv_all[0, s + 1] = jnp.zeros((rows, hd), bf16)
        kv_all[1, s + 1] = jnp.zeros((rows, hd), bf16)

    row_i = lax.broadcasted_iota(jnp.int32, (rows, rows), 0)
    col_i = lax.broadcasted_iota(jnp.int32, (rows, rows), 1)
    tril = jnp.where(col_i <= row_i, 1.0, 0.0).astype(f32)
    decay = dl_ref[...]
    cum = nt(decay, tril, lax.Precision.HIGHEST)
    cum_t = nt(tril, decay, lax.Precision.HIGHEST)
    lane = lax.broadcasted_iota(jnp.int32, (1, hd), 1) // sp

    def spread(x):
        parts = []
        for i in range(ssm_heads // per):
            v = x[:, i * per : i * per + 1]
            for k in range(1, per):
                v = jnp.where(lane == k, x[:, i * per + k : i * per + k + 1], v)
            parts.append(jnp.broadcast_to(v, (x.shape[0], hd)))
        return jnp.concatenate(parts, axis=1)

    dy = dy_ref[...]
    entry = spread(jnp.exp(cum_t))
    scaled = (dy.astype(f32) * entry).astype(bf16)
    c_val = c_ref[...]
    state_t = nn(c_val.T, scaled).astype(bf16)
    for j in range(nh):
        st_out[j, :, :width] = state_t[j * srows : (j + 1) * srows]
    whole = jnp.broadcast_to(jnp.exp(cum[:, rows - 1 : rows]), (ssm_heads, hd))
    high = whole.astype(bf16).astype(f32)
    halves = jnp.concatenate([high, whole - high], axis=0).astype(bf16)
    for j in range(nh):
        st_out[j, :, width:] = halves

    pl.semaphore_wait(barrier, n - 1 + n // 2 + hn - 2)

    def kv_copy(d, g, source, kind):
        return pltpu.make_async_remote_copy(
            src_ref=kv_ref, dst_ref=kv_all.at[kind, source],
            send_sem=kvs.at[g - base, d], recv_sem=kvr.at[kind, source],
            device_id=(d, g), device_id_type=MESH,
        )

    def forward(source, kind):
        return pltpu.make_async_remote_copy(
            src_ref=kv_all.at[kind, source], dst_ref=kv_all.at[kind, source],
            send_sem=fws.at[kind, source], recv_sem=kvr.at[kind, source],
            device_id=(sibling, h), device_id_type=MESH,
        )

    def st_copy(j, source):
        return pltpu.make_async_remote_copy(
            src_ref=st_out.at[j], dst_ref=st_in.at[source],
            send_sem=sts.at[0], recv_sem=str_.at[0],
            device_id=(j, h), device_id_type=MESH,
        )

    def inc_copy(d, source):
        return pltpu.make_async_remote_copy(
            src_ref=inc_out.at[d], dst_ref=inc_in.at[source],
            send_sem=ins.at[0], recv_sem=inr.at[0],
            device_id=(d, h), device_id_type=MESH,
        )

    @pl.loop(chip + 1, n // 2)
    def _(z):
        kv_copy(2 * z + core, h, s, parity).start()
        kv_copy(2 * z + core, mate, s, parity).start()

    kv_copy(s, mate, s, parity).start()

    @pl.when(core == 0)
    def _():
        kv_copy(sibling, h, s, parity).start()

    @pl.loop(0, nh)
    def _(j):
        @pl.when(j != s)
        def _():
            st_copy(j, s).start()

    for copy in fetch[4:]:
        copy.wait()
    for i in range(heads):
        q_i = q_ref[:, i * hd : (i + 1) * hd]
        d_i = do_ref[:, i * hd : (i + 1) * hd]
        q_st[i * rows : (i + 1) * rows] = q_i
        do_st[i * rows : (i + 1) * rows] = d_i
        q_t[:, i * rows : (i + 1) * rows] = q_i.T
        do_t[:, i * rows : (i + 1) * rows] = d_i.T

    pair = nt(b_ref[...], c_val)
    upper = col_i >= row_i
    for i in range(ssm_heads // per):
        dy_i = dy[:, i * hd : (i + 1) * hd]
        total = None
        gain = None
        for k in range(per):
            a = i * per + k
            span = jnp.where(upper, cum[a : a + 1, :] - cum_t[:, a : a + 1], -1e30)
            w = (jnp.exp(span) * pair).astype(bf16)
            r = nn(w, dy_i)
            total = r if k == 0 else jnp.where(lane == k, r, total)
            gain = (
                jnp.full((1, hd), sg_ref[a], f32) if k == 0 else jnp.where(lane == k, sg_ref[a], gain)
            )
        dx[:, i * hd : (i + 1) * hd] = total + gain * dy_i.astype(f32)

    chunks = s // 2 + 1
    key_i = lax.broadcasted_iota(jnp.int32, (chunk, cols), 0)
    query_i = s * rows + lax.rem(lax.broadcasted_iota(jnp.int32, (1, cols), 1), rows)

    def pass_on(kind):
        @pl.loop(0, chip)
        def _(z):
            kv_copy(s, h, 2 * z + core, kind).wait_recv()
            forward(2 * z + core, kind).start()

        @pl.when(parity != kind)
        def _():
            kv_copy(s, h, s, kind).wait_recv()

            @pl.when(core == 0)
            def _():
                forward(s, kind).start()

    def await_kind(kind, j):
        blk = 2 * j + 1 - core

        @pl.when(blk < s)
        def _():
            kv_copy(s, h, blk, kind).wait_recv()

    def load(kind, j):
        return kv_all[kind, pl.ds(2 * j, 2)].reshape(chunk, hd)

    def first(j, top):
        await_kind(0, j)
        sc = nn(load(0, j), q_t[...]) * scale
        sc = jnp.where(key_i + j * chunk <= query_i, sc, -1e30)
        score[j] = sc
        return jnp.maximum(top, jnp.max(sc, axis=0, keepdims=True))

    pass_on(0)
    top = lax.fori_loop(0, chunks, first, jnp.full((1, cols), -1e30, f32))
    pass_on(1)

    @pl.when(s < nh)
    def _():
        st_in[s] = st_out[jnp.minimum(s, nh - 1)]
        settle(st_in.at[pl.ds(0, n - 1)], str_.at[0])

        def one(step, inc):
            i = n - 1 - step
            inc_out[i] = inc.astype(bf16)

            @pl.when(i != s)
            def _():
                inc_copy(i, s).start()

            d = st_in[i, :, width:].astype(f32)
            d = d[:ssm_heads] + d[ssm_heads:]
            parts = []
            for a in range(ssm_heads // per):
                v = d[a * per : a * per + 1]
                for k in range(1, per):
                    v = jnp.where(lane == k, d[a * per + k : a * per + k + 1], v)
                parts.append(v)
            return st_in[i, :, :width].astype(f32) + jnp.concatenate(parts, axis=1) * inc

        lax.fori_loop(0, n, one, jnp.zeros((srows, width), f32))
        inc_in[jnp.minimum(s, nh - 1)] = inc_out[s]

    def second(j, total):
        e = jnp.exp(score[j] - top)
        score[j] = e
        return total + jnp.sum(e, axis=0, keepdims=True)

    total = lax.fori_loop(0, chunks, second, jnp.zeros((1, cols), f32))
    inv = 1.0 / total

    def dkv_copy(kind, blk, source, member):
        return pltpu.make_async_remote_copy(
            src_ref=dkv_out.at[kind, 2 * blk + core], dst_ref=dkv_in.at[source, member],
            send_sem=dks.at[kind, blk], recv_sem=dkr.at[source, member],
            device_id=(2 * blk + core, base + kind), device_id_type=MESH,
        )

    def pair_copy(kind, j):
        return pltpu.make_async_remote_copy(
            src_ref=dkv_out.at[kind, 2 * j + 1 - core], dst_ref=pair_in.at[kind, j],
            send_sem=prs.at[kind, j], recv_sem=prr.at[kind, j],
            device_id=(sibling, h), device_id_type=MESH,
        )

    def other(kind, z):
        return jnp.logical_or(z != chip, parity != kind)

    def pair_sum(kind, j):
        pair_copy(kind, j).wait_recv()
        both = dkv_part[kind, j] + pair_in[kind, j].astype(f32)
        dkv_out[kind, 2 * j + core] = both.astype(bf16)

        @pl.when(other(kind, j))
        def _():
            dkv_copy(kind, j, chip, parity).start()

    def send_grads(kind, j, val):
        low, high = val[:rows], val[rows:]
        first_core = jnp.full((1, hd), core, jnp.int32) == 0
        dkv_out[kind, 2 * j + 1 - core] = jnp.where(first_core, high, low).astype(bf16)
        pair_copy(kind, j).start()
        dkv_part[kind, j] = jnp.where(first_core, low, high)

    def third(j, out):
        await_kind(1, j)
        p = score[j] * inv
        score[j] = p
        pb = p.astype(bf16)
        send_grads(1, j, nn(pb, do_st[...]))
        return out + nn(load(1, j).T, pb)

    out_t = lax.fori_loop(0, chunks, third, jnp.zeros((hd, cols), f32))
    delta = jnp.sum(do_t[...].astype(f32) * out_t.astype(bf16).astype(f32), axis=0, keepdims=True)

    def fourth(j, dq):
        dp = nn(load(1, j), do_t[...])
        ds = (score[j] * (dp - delta)).astype(bf16)
        send_grads(0, j, nn(ds, q_st[...]) * scale)
        pair_sum(1, j)
        return dq + nn(load(0, j).T, ds)

    dq_t = lax.fori_loop(0, chunks, fourth, jnp.zeros((hd, cols), f32)) * scale

    @pl.loop(0, chunks)
    def _(j):
        pair_sum(0, j)

    @pl.when(s < nh)
    def _():
        settle(inc_in.at[pl.ds(0, nh - 1)], inr.at[0])

    @pl.when(s >= nh)
    def _():
        settle(inc_in, inr.at[0])

    carried = nn(b_ref[...], inc_in[...].reshape(nh * srows, width))
    tail = spread(jnp.exp(cum_t[rows - 1 : rows, :] - cum_t))
    dx_full = dx[...] + carried * tail
    dx[...] = dx_full

    def peak(x):
        return jnp.max(jnp.max(jnp.abs(x), axis=0, keepdims=True), axis=1, keepdims=True)

    peak_q = peak(dq_t)
    peak_x = peak(dx_full)

    def add_source(i, acc):
        for m in range(2):
            @pl.when(jnp.logical_or(i != chip, parity != m))
            def _():
                dkv_copy(parity, chip, i, m).wait_recv()

            acc = acc + dkv_in[i, m].astype(f32)
        return acc

    dkv_in[chip, parity] = dkv_out[parity, s]
    kv_grad = lax.fori_loop(chip, n // 2, add_source, jnp.zeros((rows, hd), f32))
    peak_kv = peak(kv_grad)

    sub = lax.broadcasted_iota(jnp.int32, am_out.shape, 0)
    mine = jnp.where(sub == 0, peak_q, jnp.where(sub == 1, peak_kv, peak_x))
    am_out[...] = mine
    am_in[s] = mine

    def am_copy(d, source):
        return pltpu.make_async_remote_copy(
            src_ref=am_out, dst_ref=am_in.at[source],
            send_sem=ams.at[0], recv_sem=amr.at[0],
            device_id=(d, h), device_id_type=MESH,
        )

    def am2_copy(g, source):
        return pltpu.make_async_remote_copy(
            src_ref=am2_out, dst_ref=am2_in.at[source],
            send_sem=am2s.at[0], recv_sem=am2r.at[0],
            device_id=(s, g), device_id_type=MESH,
        )

    for k in range(1, n):
        am_copy(lax.rem(s + k, n), s).start()
    settle(am_in.at[pl.ds(0, n - 1)], amr.at[0])
    column = jnp.max(am_in[...], axis=0)
    am2_out[...] = column
    am2_in[h] = column
    for k in range(1, hn):
        am2_copy(lax.rem(h + k, hn), h).start()
    settle(am2_in.at[pl.ds(0, hn - 1)], am2r.at[0])
    inverse = 1.0 / (jnp.max(am2_in[...], axis=0) + epsilon)

    scaled_q = dq_t * inverse[0:1, 0:1]
    for i in range(heads):
        gq_ref[:, i * hd : (i + 1) * hd] = scaled_q[:, i * rows : (i + 1) * rows].T.astype(bf16)
    gkv_ref[...] = (kv_grad * inverse[1:2, 0:1]).astype(bf16)
    gx_ref[...] = (dx[...] * inverse[2:3, 0:1]).astype(bf16)

    kv_copy(s, mate, s, parity).wait_send()

    @pl.when(core == 0)
    def _():
        kv_copy(sibling, h, s, parity).wait_send()
        forward(s, 1 - parity).wait_send()

    @pl.loop(chip + 1, n // 2)
    def _(z):
        kv_copy(2 * z + core, h, s, parity).wait_send()
        kv_copy(2 * z + core, mate, s, parity).wait_send()

    @pl.loop(0, chip)
    def _(z):
        forward(2 * z + core, 0).wait_send()
        forward(2 * z + core, 1).wait_send()

    @pl.when(s < nh)
    def _():
        settle(st_out.at[pl.ds(0, nh - 1)], sts.at[0])
        settle(inc_out.at[pl.ds(0, n - 1)], ins.at[0])

    @pl.when(s >= nh)
    def _():
        settle(st_out, sts.at[0])

    @pl.loop(0, chunks)
    def _(z):
        for kind in range(2):
            pair_copy(kind, z).wait_send()

            @pl.when(other(kind, z))
            def _():
                dkv_copy(kind, z, chip, parity).wait_send()

    settle(am_in.at[pl.ds(0, n - 1)], ams.at[0])
    settle(am2_in.at[pl.ds(0, hn - 1)], am2s.at[0])


def hand_over(a, b, c, x, y, z, u, v, w, in_sems, out_sems):
    hops = [
        (pltpu.make_async_copy(i, m, in_sems.at[k]), pltpu.make_async_copy(m, o, out_sems.at[k]))
        for k, (i, m, o) in enumerate(((a, u, x), (b, v, y), (c, w, z)))
    ]
    for hop in hops:
        hop[0].start()
    for hop in hops:
        hop[0].wait()
        hop[1].start()
    for hop in hops:
        hop[1].wait()


def on_device(queries, key_value, grad_out, ssm_grad, b_proj, c_proj, decay_log, skip_gain):
    n = lax.axis_size("seq")
    hn = lax.axis_size("head")
    rows, hd = key_value.shape
    heads = queries.shape[1] // hd
    cols = heads * rows
    width = ssm_grad.shape[1]
    state = b_proj.shape[1]
    ssm_heads = decay_log.shape[0]
    nh = min(n, state // 16)
    srows = state // nh
    vmem = pltpu.VMEM
    dma = pltpu.SemaphoreType.DMA
    full = pl.BlockSpec(memory_space=pltpu.VMEM)
    far = pl.BlockSpec(memory_space=pltpu.HBM)
    grads = pl.pallas_call(
        functools.partial(kernel, n, hn),
        out_shape=(
            jax.ShapeDtypeStruct(queries.shape, bf16),
            jax.ShapeDtypeStruct(key_value.shape, bf16),
            jax.ShapeDtypeStruct(ssm_grad.shape, bf16),
        ),
        in_specs=[far] * 7 + [pl.BlockSpec(memory_space=pltpu.SMEM)],
        out_specs=(full, full, full),
        scratch_shapes=[
            *(
                vmem(a.shape, a.dtype)
                for a in (queries, key_value, grad_out, ssm_grad, b_proj, c_proj, decay_log)
            ),
            vmem((2, n, rows, hd), bf16),
            vmem((cols, hd), bf16),
            vmem((hd, cols), bf16),
            vmem((cols, hd), bf16),
            vmem((hd, cols), bf16),
            vmem((n // 2, 2 * rows, cols), f32),
            vmem((2, n, rows, hd), bf16),
            vmem((n // 2, 2, rows, hd), bf16),
            vmem((2, n // 2, rows, hd), f32),
            vmem((2, n // 2, rows, hd), bf16),
            vmem((nh, srows, width + hd), bf16),
            vmem((n, srows, width + hd), bf16),
            vmem((n, srows, width), bf16),
            vmem((nh, srows, width), bf16),
            vmem((rows, width), f32),
            vmem((8, hd), f32),
            vmem((n, 8, hd), f32),
            vmem((8, hd), f32),
            vmem((hn, 8, hd), f32),
            dma((7,)), dma((2, n)),
            dma((2, n)), dma((2, n)),
            dma((2, n // 2)), dma((n // 2, 2)),
            dma((2, n // 2)), dma((2, n // 2)),
            *(dma((1,)) for _ in range(8)),
        ],
        compiler_params=pltpu.CompilerParams(
            collective_id=0, has_side_effects=True, vmem_limit_bytes=56 * 1024 * 1024
        ),
    )(queries, key_value, grad_out, ssm_grad, b_proj, c_proj, decay_log, skip_gain)
    return pl.pallas_call(
        hand_over,
        out_shape=tuple(jax.ShapeDtypeStruct(a.shape, a.dtype) for a in grads),
        in_specs=[far] * 3,
        out_specs=(far,) * 3,
        scratch_shapes=[*(vmem(a.shape, a.dtype) for a in grads), dma((3,)), dma((3,))],
        compiler_params=pltpu.CompilerParams(vmem_limit_bytes=56 * 1024 * 1024),
    )(*grads)


def solution(mesh):
    return jax.shard_map(
        on_device,
        mesh=mesh,
        in_specs=(
            P("seq", "head"),
            P("seq", "head"),
            P("seq", "head"),
            P("seq", "head"),
            P("seq", None),
            P("seq", None),
            P("head", "seq"),
            P("head"),
        ),
        out_specs=(P("seq", "head"), P("seq", "head"), P("seq", "head")),
        check_vma=False,
    )
```

```python
import functools
import math

import jax
import jax.numpy as jnp
from jax import lax
from jax.experimental import pallas as pl
from jax.experimental.pallas import tpu as pltpu
from jax.sharding import PartitionSpec as P

epsilon = 1e-06
f32 = jnp.float32
bf16 = jnp.bfloat16
MESH = pl.DeviceIdType.MESH


def nn(a, b):
    return jnp.dot(a, b, preferred_element_type=f32)


def nt(a, b, precision=None):
    return lax.dot_general(
        a, b, (((1,), (1,)), ((), ())), preferred_element_type=f32, precision=precision
    )


def kernel(
    n, hn, q_hbm, kv_hbm, do_hbm, dy_hbm, b_hbm, c_hbm, dl_hbm, sg_ref,
    gq_ref, gkv_ref, gx_ref,
    q_ref, kv_ref, do_ref, dy_ref, b_ref, c_ref, dl_ref,
    kv_all, q_st, q_t, do_st, do_t, score, dkv_out, dkv_in, dkv_part, pair_in,
    st_out, st_in, inc_out, inc_in, dx, am_out, am_in, am2_out, am2_in,
    loads, fws, kvs, kvr, dks, dkr, prs, prr, sts, str_, ins, inr, ams, amr, am2s, am2r,
):
    s = lax.axis_index("seq")
    h = lax.axis_index("head")
    parity = lax.rem(h, 2)
    base = h - parity
    mate = base + 1 - parity
    rows, hd = kv_ref.shape
    heads = q_ref.shape[1] // hd
    cols = heads * rows
    scale = 1.0 / math.sqrt(hd)
    nh, srows = st_out.shape[:2]
    ssm_heads = dl_ref.shape[0]
    width = dy_ref.shape[1]
    sp = width // ssm_heads
    per = hd // sp
    chunk = 2 * rows
    core = lax.rem(s, 2)
    chip = s // 2
    sibling = s + 1 - 2 * core

    fetch = [
        pltpu.make_async_copy(a, b, loads.at[i])
        for i, (a, b) in enumerate((
            (dl_hbm, dl_ref), (dy_hbm, dy_ref), (c_hbm, c_ref), (kv_hbm, kv_ref),
            (b_hbm, b_ref), (q_hbm, q_ref), (do_hbm, do_ref),
        ))
    ]
    for copy in fetch:
        copy.start()
    barrier = pltpu.get_barrier_semaphore()

    for k in range(1, n):
        pl.semaphore_signal(
            barrier, inc=1, device_id=(lax.rem(s + k, n), h), device_id_type=MESH
        )
    for k in range(0, n, 2):
        pl.semaphore_signal(
            barrier, inc=1, device_id=(lax.rem(s + k, n), mate), device_id_type=MESH
        )
    for k in range(2, hn):
        g = lax.rem(base + k, hn)
        pl.semaphore_signal(barrier, inc=1, device_id=(s, g), device_id_type=MESH)

    def settle(ref, sem):
        pltpu.make_async_copy(ref, ref, sem).wait()

    for copy in fetch[:4]:
        copy.wait()
    kv_all[parity, s] = kv_ref[...]

    @pl.when(jnp.logical_and(lax.rem(s, 2) == 0, s + 1 < n))
    def _():
        kv_all[0, s + 1] = jnp.zeros((rows, hd), bf16)
        kv_all[1, s + 1] = jnp.zeros((rows, hd), bf16)

    row_i = lax.broadcasted_iota(jnp.int32, (rows, rows), 0)
    col_i = lax.broadcasted_iota(jnp.int32, (rows, rows), 1)
    tril = jnp.where(col_i <= row_i, 1.0, 0.0).astype(f32)
    decay = dl_ref[...]
    cum = nt(decay, tril, lax.Precision.HIGHEST)
    cum_t = nt(tril, decay, lax.Precision.HIGHEST)
    lane = lax.broadcasted_iota(jnp.int32, (1, hd), 1) // sp

    def spread(x):
        parts = []
        for i in range(ssm_heads // per):
            v = x[:, i * per : i * per + 1]
            for k in range(1, per):
                v = jnp.where(lane == k, x[:, i * per + k : i * per + k + 1], v)
            parts.append(jnp.broadcast_to(v, (x.shape[0], hd)))
        return jnp.concatenate(parts, axis=1)

    dy = dy_ref[...]
    entry = spread(jnp.exp(cum_t))
    scaled = (dy.astype(f32) * entry).astype(bf16)
    c_val = c_ref[...]
    state_t = nn(c_val.T, scaled).astype(bf16)
    for j in range(nh):
        st_out[j, :, :width] = state_t[j * srows : (j + 1) * srows]
    whole = jnp.broadcast_to(jnp.exp(cum[:, rows - 1 : rows]), (ssm_heads, hd))
    high = whole.astype(bf16).astype(f32)
    halves = jnp.concatenate([high, whole - high], axis=0).astype(bf16)
    for j in range(nh):
        st_out[j, :, width:] = halves

    pl.semaphore_wait(barrier, n - 1 + n // 2 + hn - 2)

    def kv_copy(d, g, source, kind):
        return pltpu.make_async_remote_copy(
            src_ref=kv_ref, dst_ref=kv_all.at[kind, source],
            send_sem=kvs.at[g - base, d], recv_sem=kvr.at[kind, source],
            device_id=(d, g), device_id_type=MESH,
        )

    def forward(source, kind):
        return pltpu.make_async_remote_copy(
            src_ref=kv_all.at[kind, source], dst_ref=kv_all.at[kind, source],
            send_sem=fws.at[kind, source], recv_sem=kvr.at[kind, source],
            device_id=(sibling, h), device_id_type=MESH,
        )

    def st_copy(j, source):
        return pltpu.make_async_remote_copy(
            src_ref=st_out.at[j], dst_ref=st_in.at[source],
            send_sem=sts.at[0], recv_sem=str_.at[0],
            device_id=(j, h), device_id_type=MESH,
        )

    def inc_copy(d, source):
        return pltpu.make_async_remote_copy(
            src_ref=inc_out.at[d], dst_ref=inc_in.at[source],
            send_sem=ins.at[0], recv_sem=inr.at[0],
            device_id=(d, h), device_id_type=MESH,
        )

    @pl.loop(chip + 1, n // 2)
    def _(z):
        kv_copy(2 * z + core, h, s, parity).start()
        kv_copy(2 * z + core, mate, s, parity).start()

    kv_copy(s, mate, s, parity).start()

    @pl.when(core == 0)
    def _():
        kv_copy(sibling, h, s, parity).start()

    @pl.loop(0, nh)
    def _(j):
        @pl.when(j != s)
        def _():
            st_copy(j, s).start()

    for copy in fetch[4:]:
        copy.wait()
    for i in range(heads):
        q_i = q_ref[:, i * hd : (i + 1) * hd]
        d_i = do_ref[:, i * hd : (i + 1) * hd]
        q_st[i * rows : (i + 1) * rows] = q_i
        do_st[i * rows : (i + 1) * rows] = d_i
        q_t[:, i * rows : (i + 1) * rows] = q_i.T
        do_t[:, i * rows : (i + 1) * rows] = d_i.T

    pair = nt(b_ref[...], c_val)
    upper = col_i >= row_i
    for i in range(ssm_heads // per):
        dy_i = dy[:, i * hd : (i + 1) * hd]
        total = None
        gain = None
        for k in range(per):
            a = i * per + k
            span = jnp.where(upper, cum[a : a + 1, :] - cum_t[:, a : a + 1], -1e30)
            w = (jnp.exp(span) * pair).astype(bf16)
            r = nn(w, dy_i)
            total = r if k == 0 else jnp.where(lane == k, r, total)
            gain = (
                jnp.full((1, hd), sg_ref[a], f32) if k == 0 else jnp.where(lane == k, sg_ref[a], gain)
            )
        dx[:, i * hd : (i + 1) * hd] = total + gain * dy_i.astype(f32)

    chunks = s // 2 + 1
    key_i = lax.broadcasted_iota(jnp.int32, (chunk, cols), 0)
    query_i = s * rows + lax.rem(lax.broadcasted_iota(jnp.int32, (1, cols), 1), rows)

    def pass_on(kind):
        @pl.loop(0, chip)
        def _(z):
            kv_copy(s, h, 2 * z + core, kind).wait_recv()
            forward(2 * z + core, kind).start()

        @pl.when(parity != kind)
        def _():
            kv_copy(s, h, s, kind).wait_recv()

            @pl.when(core == 0)
            def _():
                forward(s, kind).start()

    def await_kind(kind, j):
        blk = 2 * j + 1 - core

        @pl.when(blk < s)
        def _():
            kv_copy(s, h, blk, kind).wait_recv()

    def load(kind, j):
        return kv_all[kind, pl.ds(2 * j, 2)].reshape(chunk, hd)

    def first(j, top):
        await_kind(0, j)
        sc = nn(load(0, j), q_t[...]) * scale
        sc = jnp.where(key_i + j * chunk <= query_i, sc, -1e30)
        score[j] = sc
        return jnp.maximum(top, jnp.max(sc, axis=0, keepdims=True))

    pass_on(0)
    top = lax.fori_loop(0, chunks, first, jnp.full((1, cols), -1e30, f32))
    @pl.when(s < nh)
    def _():
        st_in[s] = st_out[jnp.minimum(s, nh - 1)]
        settle(st_in.at[pl.ds(0, n - 1)], str_.at[0])

        def one(step, inc):
            i = n - 1 - step
            inc_out[i] = inc.astype(bf16)

            @pl.when(i != s)
            def _():
                inc_copy(i, s).start()

            d = st_in[i, :, width:].astype(f32)
            d = d[:ssm_heads] + d[ssm_heads:]
            parts = []
            for a in range(ssm_heads // per):
                v = d[a * per : a * per + 1]
                for k in range(1, per):
                    v = jnp.where(lane == k, d[a * per + k : a * per + k + 1], v)
                parts.append(v)
            return st_in[i, :, :width].astype(f32) + jnp.concatenate(parts, axis=1) * inc

        lax.fori_loop(0, n, one, jnp.zeros((srows, width), f32))
        inc_in[jnp.minimum(s, nh - 1)] = inc_out[s]

    pass_on(1)

    def second(j, total):
        e = jnp.exp(score[j] - top)
        score[j] = e
        return total + jnp.sum(e, axis=0, keepdims=True)

    total = lax.fori_loop(0, chunks, second, jnp.zeros((1, cols), f32))
    inv = 1.0 / total

    def dkv_copy(kind, blk, source, member):
        return pltpu.make_async_remote_copy(
            src_ref=dkv_out.at[kind, 2 * blk + core], dst_ref=dkv_in.at[source, member],
            send_sem=dks.at[kind, blk], recv_sem=dkr.at[source, member],
            device_id=(2 * blk + core, base + kind), device_id_type=MESH,
        )

    def pair_copy(kind, j):
        return pltpu.make_async_remote_copy(
            src_ref=dkv_out.at[kind, 2 * j + 1 - core], dst_ref=pair_in.at[kind, j],
            send_sem=prs.at[kind, j], recv_sem=prr.at[kind, j],
            device_id=(sibling, h), device_id_type=MESH,
        )

    def other(kind, z):
        return jnp.logical_or(z != chip, parity != kind)

    def pair_sum(kind, j):
        pair_copy(kind, j).wait_recv()
        both = dkv_part[kind, j] + pair_in[kind, j].astype(f32)
        dkv_out[kind, 2 * j + core] = both.astype(bf16)

        @pl.when(other(kind, j))
        def _():
            dkv_copy(kind, j, chip, parity).start()

    def send_grads(kind, j, val):
        low, high = val[:rows], val[rows:]
        first_core = jnp.full((1, hd), core, jnp.int32) == 0
        dkv_out[kind, 2 * j + 1 - core] = jnp.where(first_core, high, low).astype(bf16)
        pair_copy(kind, j).start()
        dkv_part[kind, j] = jnp.where(first_core, low, high)

    def third(j, out):
        await_kind(1, j)
        p = score[j] * inv
        score[j] = p
        pb = p.astype(bf16)
        send_grads(1, j, nn(pb, do_st[...]))
        return out + nn(load(1, j).T, pb)

    out_t = lax.fori_loop(0, chunks, third, jnp.zeros((hd, cols), f32))
    delta = jnp.sum(do_t[...].astype(f32) * out_t.astype(bf16).astype(f32), axis=0, keepdims=True)

    def fourth(j, dq):
        dp = nn(load(1, j), do_t[...])
        ds = (score[j] * (dp - delta)).astype(bf16)
        send_grads(0, j, nn(ds, q_st[...]) * scale)
        pair_sum(1, j)
        return dq + nn(load(0, j).T, ds)

    dq_t = lax.fori_loop(0, chunks, fourth, jnp.zeros((hd, cols), f32)) * scale

    @pl.loop(0, chunks)
    def _(j):
        pair_sum(0, j)

    @pl.when(s < nh)
    def _():
        settle(inc_in.at[pl.ds(0, nh - 1)], inr.at[0])

    @pl.when(s >= nh)
    def _():
        settle(inc_in, inr.at[0])

    carried = nn(b_ref[...], inc_in[...].reshape(nh * srows, width))
    tail = spread(jnp.exp(cum_t[rows - 1 : rows, :] - cum_t))
    dx_full = dx[...] + carried * tail
    dx[...] = dx_full

    def peak(x):
        return jnp.max(jnp.max(jnp.abs(x), axis=0, keepdims=True), axis=1, keepdims=True)

    peak_q = peak(dq_t)
    peak_x = peak(dx_full)

    def add_source(i, acc):
        for m in range(2):
            @pl.when(jnp.logical_or(i != chip, parity != m))
            def _():
                dkv_copy(parity, chip, i, m).wait_recv()

            acc = acc + dkv_in[i, m].astype(f32)
        return acc

    dkv_in[chip, parity] = dkv_out[parity, s]
    kv_grad = lax.fori_loop(chip, n // 2, add_source, jnp.zeros((rows, hd), f32))
    peak_kv = peak(kv_grad)

    sub = lax.broadcasted_iota(jnp.int32, am_out.shape, 0)
    mine = jnp.where(sub == 0, peak_q, jnp.where(sub == 1, peak_kv, peak_x))
    am_out[...] = mine
    am_in[s] = mine

    def am_copy(d, source):
        return pltpu.make_async_remote_copy(
            src_ref=am_out, dst_ref=am_in.at[source],
            send_sem=ams.at[0], recv_sem=amr.at[0],
            device_id=(d, h), device_id_type=MESH,
        )

    def am2_copy(g, source):
        return pltpu.make_async_remote_copy(
            src_ref=am2_out, dst_ref=am2_in.at[source],
            send_sem=am2s.at[0], recv_sem=am2r.at[0],
            device_id=(s, g), device_id_type=MESH,
        )

    for k in range(1, n):
        am_copy(lax.rem(s + k, n), s).start()
    settle(am_in.at[pl.ds(0, n - 1)], amr.at[0])
    column = jnp.max(am_in[...], axis=0)
    am2_out[...] = column
    am2_in[h] = column
    for k in range(1, hn):
        am2_copy(lax.rem(h + k, hn), h).start()
    settle(am2_in.at[pl.ds(0, hn - 1)], am2r.at[0])
    inverse = 1.0 / (jnp.max(am2_in[...], axis=0) + epsilon)

    scaled_q = dq_t * inverse[0:1, 0:1]
    for i in range(heads):
        gq_ref[:, i * hd : (i + 1) * hd] = scaled_q[:, i * rows : (i + 1) * rows].T.astype(bf16)
    gkv_ref[...] = (kv_grad * inverse[1:2, 0:1]).astype(bf16)
    gx_ref[...] = (dx[...] * inverse[2:3, 0:1]).astype(bf16)

    kv_copy(s, mate, s, parity).wait_send()

    @pl.when(core == 0)
    def _():
        kv_copy(sibling, h, s, parity).wait_send()
        forward(s, 1 - parity).wait_send()

    @pl.loop(chip + 1, n // 2)
    def _(z):
        kv_copy(2 * z + core, h, s, parity).wait_send()
        kv_copy(2 * z + core, mate, s, parity).wait_send()

    @pl.loop(0, chip)
    def _(z):
        forward(2 * z + core, 0).wait_send()
        forward(2 * z + core, 1).wait_send()

    @pl.when(s < nh)
    def _():
        settle(st_out.at[pl.ds(0, nh - 1)], sts.at[0])
        settle(inc_out.at[pl.ds(0, n - 1)], ins.at[0])

    @pl.when(s >= nh)
    def _():
        settle(st_out, sts.at[0])

    @pl.loop(0, chunks)
    def _(z):
        for kind in range(2):
            pair_copy(kind, z).wait_send()

            @pl.when(other(kind, z))
            def _():
                dkv_copy(kind, z, chip, parity).wait_send()

    settle(am_in.at[pl.ds(0, n - 1)], ams.at[0])
    settle(am2_in.at[pl.ds(0, hn - 1)], am2s.at[0])


def hand_over(a, b, c, x, y, z, u, v, w, in_sems, out_sems):
    hops = [
        (pltpu.make_async_copy(i, m, in_sems.at[k]), pltpu.make_async_copy(m, o, out_sems.at[k]))
        for k, (i, m, o) in enumerate(((a, u, x), (b, v, y), (c, w, z)))
    ]
    for hop in hops:
        hop[0].start()
    for hop in hops:
        hop[0].wait()
        hop[1].start()
    for hop in hops:
        hop[1].wait()


def on_device(queries, key_value, grad_out, ssm_grad, b_proj, c_proj, decay_log, skip_gain):
    n = lax.axis_size("seq")
    hn = lax.axis_size("head")
    rows, hd = key_value.shape
    heads = queries.shape[1] // hd
    cols = heads * rows
    width = ssm_grad.shape[1]
    state = b_proj.shape[1]
    ssm_heads = decay_log.shape[0]
    nh = min(n, state // 16)
    srows = state // nh
    vmem = pltpu.VMEM
    dma = pltpu.SemaphoreType.DMA
    full = pl.BlockSpec(memory_space=pltpu.VMEM)
    far = pl.BlockSpec(memory_space=pltpu.HBM)
    grads = pl.pallas_call(
        functools.partial(kernel, n, hn),
        out_shape=(
            jax.ShapeDtypeStruct(queries.shape, bf16),
            jax.ShapeDtypeStruct(key_value.shape, bf16),
            jax.ShapeDtypeStruct(ssm_grad.shape, bf16),
        ),
        in_specs=[far] * 7 + [pl.BlockSpec(memory_space=pltpu.SMEM)],
        out_specs=(full, full, full),
        scratch_shapes=[
            *(
                vmem(a.shape, a.dtype)
                for a in (queries, key_value, grad_out, ssm_grad, b_proj, c_proj, decay_log)
            ),
            vmem((2, n, rows, hd), bf16),
            vmem((cols, hd), bf16),
            vmem((hd, cols), bf16),
            vmem((cols, hd), bf16),
            vmem((hd, cols), bf16),
            vmem((n // 2, 2 * rows, cols), f32),
            vmem((2, n, rows, hd), bf16),
            vmem((n // 2, 2, rows, hd), bf16),
            vmem((2, n // 2, rows, hd), f32),
            vmem((2, n // 2, rows, hd), bf16),
            vmem((nh, srows, width + hd), bf16),
            vmem((n, srows, width + hd), bf16),
            vmem((n, srows, width), bf16),
            vmem((nh, srows, width), bf16),
            vmem((rows, width), f32),
            vmem((8, hd), f32),
            vmem((n, 8, hd), f32),
            vmem((8, hd), f32),
            vmem((hn, 8, hd), f32),
            dma((7,)), dma((2, n)),
            dma((2, n)), dma((2, n)),
            dma((2, n // 2)), dma((n // 2, 2)),
            dma((2, n // 2)), dma((2, n // 2)),
            *(dma((1,)) for _ in range(8)),
        ],
        compiler_params=pltpu.CompilerParams(
            collective_id=0, has_side_effects=True, vmem_limit_bytes=56 * 1024 * 1024
        ),
    )(queries, key_value, grad_out, ssm_grad, b_proj, c_proj, decay_log, skip_gain)
    return pl.pallas_call(
        hand_over,
        out_shape=tuple(jax.ShapeDtypeStruct(a.shape, a.dtype) for a in grads),
        in_specs=[far] * 3,
        out_specs=(far,) * 3,
        scratch_shapes=[*(vmem(a.shape, a.dtype) for a in grads), dma((3,)), dma((3,))],
        compiler_params=pltpu.CompilerParams(vmem_limit_bytes=56 * 1024 * 1024),
    )(*grads)


def solution(mesh):
    return jax.shard_map(
        on_device,
        mesh=mesh,
        in_specs=(
            P("seq", "head"),
            P("seq", "head"),
            P("seq", "head"),
            P("seq", "head"),
            P("seq", None),
            P("seq", None),
            P("head", "seq"),
            P("head"),
        ),
        out_specs=(P("seq", "head"), P("seq", "head"), P("seq", "head")),
        check_vma=False,
    )
```
